1024 devices in a mesh: outer: 64 (over z_lo, y, core), inner: 16 (over x, z_hi).
Axes of the slice: x: 8, y: 8, z: 8 (z_hi: 2, z_lo: 4; z = z_hi * 4 + z_lo), core: 2. Of those that a mesh axis runs over, the one named last changes fastest.
Arguments:
- hidden: bfloat16 [4096, 14336], P('inner', 'outer'), may hold values from -6 to 6
- grad_out: bfloat16 [4096, 6144], P('inner', 'outer'), may hold values from -0.29882812 to 0.29882812
- codes: bfloat16 [14336, 6144], P('outer', 'inner'), may hold values from -4 to 4
- scales: float32 [14336, 48], P('outer', 'inner'), may hold values from 0.1 to 0.6
Outputs:
- grad_hidden: bfloat16 [4096, 14336], P('inner', 'outer')
- grad_weight: float32 [14336, 6144], P('outer', 'inner')
The draws below stay inside these ranges and needn't reach their ends.
All inputs are finite; a program needn't handle non-finite values.
Results may differ from the reference program's by a relative error of at most 0.017.
Values may be sent and summed in bfloat16 or wider, within the bound.
A program may use at most 32 MiB of HBM per device.

```python
import math
import jax
import jax.numpy as jnp
from jax import lax

D = 6144
FF = 14336
BLK = 128
TOK_DEV = 256
TOKENS = 4096


def block_scale(own_key, extent, shards, least, high):
    gain = 1.0
    for axis_at, parts in shards:
        draws = jax.random.uniform(jax.random.fold_in(jax.random.fold_in(own_key, 6), axis_at), (parts,), jnp.float32, least / len(shards), high / len(shards))
        gain = gain * jnp.repeat(jnp.exp(draws), extent[axis_at] // parts).reshape((-1,) + (1,) * (len(extent) - 1 - axis_at))
    return gain


def normal_values(rng, dims, deviation, bound, pieces=(), kind=jnp.bfloat16):
    values = jax.random.normal(rng, dims, jnp.float32) * deviation
    if len(pieces) > 0:
        values = block_scale(rng, dims, pieces, -0.22, 0.18) * values
    return jnp.clip(values, min=-bound, max=bound).astype(kind)


def setup_inputs(seed: int = 0) -> dict:
    key_list = jax.random.split(jax.random.key(seed), 5)
    hidden = normal_values(key_list[0], (TOKENS, FF), 1.0, 6.0, ((0, 16), (1, 64)))
    grad_out = normal_values(key_list[1], (TOKENS, D), 0.05, 0.29882812, ((0, 16), (1, 64)))
    codes = normal_values(key_list[2], (FF, D), 1.0, 4.0, ((0, 64), (1, 16)))
    scales = jnp.clip(jnp.exp(math.log(0.6) - 1.7917595 * jax.random.uniform(key_list[3], (FF, D // BLK), jnp.float32) ** block_scale(key_list[3], (FF, D // BLK), ((0, 64), (1, 16)), -0.2, 0.2)), 0.1, 0.6)
    return dict(hidden=hidden, grad_out=grad_out, codes=codes, scales=scales)


def reference(hidden, grad_out, codes, scales):
    weight = (codes.astype(jnp.float32) * jnp.repeat(scales, BLK, axis=1)).astype(jnp.bfloat16)
    grad_hidden = lax.dot_general(grad_out, weight, (((1,), (1,)), ((), ())), preferred_element_type=jnp.float32).astype(jnp.bfloat16)
    groups = TOKENS // TOK_DEV

    def add_group(total, index):
        start = (index * TOK_DEV).astype(jnp.int32)
        rows_h = lax.dynamic_slice_in_dim(hidden, start, TOK_DEV, 0)
        rows_g = lax.dynamic_slice_in_dim(grad_out, start, TOK_DEV, 0)
        partial_term = lax.dot_general(rows_h, rows_g, (((0,), (0,)), ((), ())), preferred_element_type=jnp.float32).astype(jnp.bfloat16)
        partial_term = lax.optimization_barrier(partial_term)
        return total + partial_term.astype(jnp.float32), None

    grad_weight, _ = lax.scan(add_group, jnp.zeros((FF, D), jnp.float32), jnp.arange(groups, dtype=jnp.int32))
    return grad_hidden, grad_weight
```

```python
import jax
import jax.numpy as jnp
from jax import lax
from jax.experimental import pallas as pl
from jax.experimental.pallas import tpu as pltpu
from jax.sharding import PartitionSpec as P

BLK = 128
X, HZ, ZL, Y = 8, 2, 4, 8
TOK, FFD, GCOL, WCOL = 256, 224, 96, 384
MESH = pl.DeviceIdType.MESH
F32, BF16 = jnp.float32, jnp.bfloat16


def kernel(
    ht, gt, codes, scales, ght, gw,
    g, hb, w, acc, p, rs_out, rs_in, gw_out, gw_in,
    perm_s, perm_r, z_s, z_r, y_s, y_r, sib_s, sib_r, h_s, h_r, w_s, w_r, rs_s, rs_r, gw_s, gw_r,
):
    o = lax.axis_index("outer")
    i = lax.axis_index("inner")
    c = lax.rem(o, 2)
    y = lax.rem(o // 2, Y)
    zl = o // (2 * Y)
    x = i // HZ
    h = lax.rem(i, HZ)
    sgn = 1 - 2 * c

    def dev(x_, h_, zl_, y_, c_):
        return {"outer": zl_ * (2 * Y) + y_ * 2 + c_, "inner": x_ * HZ + h_}

    def mod(a, n):
        return lax.rem(a + n, n)

    perm_to = dev(2 * zl + y // 4, h, mod(lax.rem(y, 4) + 2, 4), x, c)
    perm_from = dev(y, h, x // 2, lax.rem(x, 2) * 4 + mod(zl + 2, 4), c)
    z_peer = [dev(x, h, mod(zl + r, ZL), y, c) for r in range(1, ZL)]
    sibling = dev(x, h, zl, y, 1 - c)
    y_long, y_short = dev(x, h, zl, mod(y + sgn, Y), c), dev(x, h, zl, mod(y - sgn, Y), c)
    x_long, x_short = dev(mod(x + sgn, X), h, zl, y, c), dev(mod(x - sgn, X), h, zl, y, c)
    h_peer = dev(x, 1 - h, zl, y, c)
    peers = [perm_to, perm_from, *z_peer, sibling, y_long, y_short, x_long, x_short, h_peer]

    barrier = pltpu.get_barrier_semaphore()
    for peer in peers:
        pl.semaphore_signal(barrier, inc=1, device_id=peer, device_id_type=MESH)

    for b in range(WCOL // BLK):
        cols = slice(b * BLK, (b + 1) * BLK)
        scale = jnp.broadcast_to(scales[b : b + 1, :], (BLK, FFD)).T
        w[h, :, cols] = (codes[:, cols].astype(F32) * scale).astype(BF16)
    hb[x] = ht[...]

    pl.semaphore_wait(barrier, len(peers))

    sends = []

    def copy(src, dst, s, r, to):
        return pltpu.make_async_remote_copy(
            src_ref=src, dst_ref=dst, send_sem=s, recv_sem=r, device_id=to, device_id_type=MESH
        )

    def start(cp):
        cp.start()
        sends.append(cp)

    def chunk(t, k):
        return g.at[t, mod(zl + 2 - k, 4), c]

    def y_block(d, s):
        return mod(y - sgn * s, Y) if d == 0 else mod(y + sgn * s, Y)

    def x_block(d, s):
        return mod(x - sgn * s, X) if d == 0 else mod(x + sgn * s, X)

    def ring(d, s, k):
        ref = chunk(y_block(d, s), k)
        return copy(ref, ref, y_s.at[d, s, k], y_r.at[d, s, k], y_long if d == 0 else y_short)

    def sib(t, k):
        ref = chunk(t, k)
        return copy(ref, ref, sib_s.at[t, k], sib_r.at[t, k], sibling)

    def hcopy(d, s):
        ref = hb.at[x_block(d, s)]
        return copy(ref, ref, h_s.at[d, s], h_r.at[d, s], x_long if d == 0 else x_short)

    steps = (4, 3)

    def h_step(s):
        for d in (0, 1):
            if s < steps[d]:
                hcopy(d, s).wait_recv()
                if s + 1 < steps[d]:
                    start(hcopy(d, s + 1))

    perm = copy(gt, g.at[x, lax.rem(y, 4), c], perm_s, perm_r, perm_to)
    start(perm)
    for d in (0, 1):
        start(hcopy(d, 0))

    def zcopy(k):
        ref = chunk(y, 0)
        return copy(ref, ref, z_s.at[k - 1], z_r.at[k - 1], z_peer[k - 1])

    for k in range(4):
        if k == 0:
            perm.wait_recv()
            for r in range(1, 4):
                start(zcopy(r))
        else:
            zcopy(k).wait_recv()
        start(ring(0, 0, k))
        start(ring(1, 0, k))
        start(sib(y, k))
        if k == 0:
            h_step(0)
    w_copy = copy(w.at[h], w.at[h], w_s, w_r, h_peer)
    start(w_copy)
    h_step(1)

    def grad_hidden(t):
        for k in range(4):
            sib(t, k).wait_recv()
        r = lax.dot_general(
            w[0], g[t, 0:2].reshape(WCOL, TOK), (((1,), (0,)), ((), ())), preferred_element_type=F32
        )
        p[t] = r + lax.dot_general(
            w[1], g[t, 2:4].reshape(WCOL, TOK), (((1,), (0,)), ((), ())), preferred_element_type=F32
        )

    def grad_weight(t, first=False):
        for n in range(2):
            r = lax.dot_general(
                hb[t],
                g[t, 2 * n : 2 * n + 2].reshape(WCOL, TOK),
                (((1,), (1,)), ((), ())),
                preferred_element_type=F32,
            )
            if first:
                acc[n] = r
            else:
                acc[n] += r

    def at_distance(s):
        return [y_block(0, s)] if s in (0, 4) else [y_block(0, s), y_block(1, s)]

    for s in range(4):
        for k in range(4):
            for d in (0, 1):
                if s < steps[d]:
                    ring(d, s, k).wait_recv()
                    if s + 1 < steps[d]:
                        start(ring(d, s + 1, k))
                    start(sib(y_block(d, s + 1), k))
        if s < 2:
            h_step(s + 2)
        if s == 1:
            w_copy.wait_recv()
            for t in at_distance(0) + at_distance(1):
                grad_hidden(t)
            grad_weight(y, True)
            for t in at_distance(1):
                grad_weight(t)
        if s >= 2:
            for t in at_distance(s):
                grad_hidden(t)
                grad_weight(t)
    grad_hidden(y_block(0, 4))
    grad_weight(y_block(0, 4))

    gw_out[...] = acc[1 - h].astype(BF16)
    gw_copy = copy(gw_out, gw_in, gw_s, gw_r, h_peer)
    start(gw_copy)

    half = FFD // 2

    def rs(d, e, q):
        rows = pl.ds(q * half, half)
        return copy(
            rs_out.at[d, e, rows], rs_in.at[d, e, rows], rs_s.at[d, e, q], rs_r.at[d, e, q],
            x_long if d == 0 else x_short,
        )

    for e in range(4):
        for q in range(2):
            rows = pl.ds(q * half, half)
            for d in (0, 1):
                if e < steps[d]:
                    b = mod(x + sgn * (4 - e), X) if d == 0 else mod(x - sgn * (3 - e), X)
                    v = p[b, rows]
                    if e > 0:
                        rs(d, e - 1, q).wait_recv()
                        v = v + rs_in[d, e - 1, rows].astype(F32)
                    rs_out[d, e, rows] = v.astype(BF16)
                    start(rs(d, e, q))
    for q in range(2):
        rows = pl.ds(q * half, half)
        rs(1, 2, q).wait_recv()
        v = p[x, rows] + rs_in[1, 2, rows].astype(F32)
        rs(0, 3, q).wait_recv()
        ght[rows] = (v + rs_in[0, 3, rows].astype(F32)).astype(BF16)
    gw_copy.wait_recv()
    gw[...] = acc[h] + gw_in[...].astype(F32)
    for cp in sends:
        cp.wait_send()


def shards(hidden, grad_out, codes, scales):
    vmem = pl.BlockSpec(memory_space=pltpu.VMEM)
    dma = pltpu.SemaphoreType.DMA
    ght, gw = pl.pallas_call(
        kernel,
        out_shape=(
            jax.ShapeDtypeStruct((FFD, TOK), BF16),
            jax.ShapeDtypeStruct((FFD, WCOL), F32),
        ),
        in_specs=[vmem] * 4,
        out_specs=(vmem, vmem),
        scratch_shapes=[
            pltpu.VMEM((Y, 4, 2, GCOL, TOK), BF16),
            pltpu.VMEM((X, FFD, TOK), BF16),
            pltpu.VMEM((2, FFD, WCOL), BF16),
            pltpu.VMEM((2, FFD, WCOL), F32),
            pltpu.VMEM((X, FFD, TOK), F32),
            pltpu.VMEM((2, 4, FFD, TOK), BF16),
            pltpu.VMEM((2, 4, FFD, TOK), BF16),
            pltpu.VMEM((FFD, WCOL), BF16),
            pltpu.VMEM((FFD, WCOL), BF16),
            dma, dma,
            dma((3,)), dma((3,)),
            dma((2, 4, 4)), dma((2, 4, 4)),
            dma((8, 4)), dma((8, 4)),
            dma((2, 4)), dma((2, 4)),
            dma, dma,
            dma((2, 4, 2)), dma((2, 4, 2)),
            dma, dma,
        ],
        compiler_params=pltpu.CompilerParams(
            collective_id=0, has_side_effects=True, vmem_limit_bytes=40 * 2**20
        ),
        name="fused",
    )(hidden.T, grad_out.T, codes, scales.T)
    return ght.T, gw


def solution(mesh):
    return jax.shard_map(
        shards,
        mesh=mesh,
        in_specs=(
            P("inner", "outer"),
            P("inner", "outer"),
            P("outer", "inner"),
            P("outer", "inner"),
        ),
        out_specs=(P("inner", "outer"), P("outer", "inner")),
        check_vma=False,
    )
```

```python
import jax
import jax.numpy as jnp
from jax import lax
from jax.experimental import pallas as pl
from jax.experimental.pallas import tpu as pltpu
from jax.sharding import PartitionSpec as P

BLK = 128
X, HZ, ZL, Y = 8, 2, 4, 8
TOK, FFD, GCOL, WCOL = 256, 224, 96, 384
MESH = pl.DeviceIdType.MESH
F32, BF16 = jnp.float32, jnp.bfloat16


def kernel(
    ht, gt, codes, scales, ght, gw,
    g, hb, cv, sv, w, acc, p, rs_out, pair_in, own_in, gw_out, gw_in,
    in_s, perm_s, perm_r, z_s, z_r, y_s, y_r, sib_s, sib_r, last_s, last_r, h_s, h_r, w_s, w_r, rs_s, pair_r, own_r, gw_s, gw_r,
):
    o = lax.axis_index("outer")
    i = lax.axis_index("inner")
    c = lax.rem(o, 2)
    y = lax.rem(o // 2, Y)
    zl = o // (2 * Y)
    x = i // HZ
    h = lax.rem(i, HZ)
    sgn = 1 - 2 * c

    def dev(x_, h_, zl_, y_, c_):
        return {"outer": zl_ * (2 * Y) + y_ * 2 + c_, "inner": x_ * HZ + h_}

    def mod(a, n):
        return lax.rem(a + n, n)

    perm_to = dev(2 * zl + y // 4, h, mod(lax.rem(y, 4) + 2, 4), x, c)
    perm_from = dev(y, h, x // 2, lax.rem(x, 2) * 4 + mod(zl + 2, 4), c)
    z_peer = [dev(x, h, mod(zl + r, ZL), y, c) for r in range(1, ZL)]
    sibling = dev(x, h, zl, y, 1 - c)
    y_long, y_short = dev(x, h, zl, mod(y + sgn, Y), c), dev(x, h, zl, mod(y - sgn, Y), c)
    x_long, x_short = dev(mod(x + sgn, X), h, zl, y, c), dev(mod(x - sgn, X), h, zl, y, c)
    h_peer = dev(x, 1 - h, zl, y, c)
    x_far = [dev(mod(x + n * sgn, X), h, zl, y, c) for n in (3, -3, 2, -2)]
    peers = [perm_to, perm_from, *z_peer, sibling, y_long, y_short, x_long, x_short, *x_far, h_peer]

    barrier = pltpu.get_barrier_semaphore()
    for peer in peers:
        pl.semaphore_signal(barrier, inc=1, device_id=peer, device_id_type=MESH)

    loads = [
        pltpu.make_async_copy(codes, cv, in_s.at[0]),
        pltpu.make_async_copy(scales, sv, in_s.at[1]),
        pltpu.make_async_copy(ht, hb.at[x], in_s.at[2]),
    ]
    for load in loads:
        load.start()

    pl.semaphore_wait(barrier, len(peers))

    sends = []

    def copy(src, dst, s, r, to):
        return pltpu.make_async_remote_copy(
            src_ref=src, dst_ref=dst, send_sem=s, recv_sem=r, device_id=to, device_id_type=MESH
        )

    def start(cp):
        cp.start()
        sends.append(cp)

    def chunk(t, k):
        return g.at[t, mod(zl + 2 - k, 4), c]

    def y_block(d, s):
        return mod(y - sgn * s, Y) if d == 0 else mod(y + sgn * s, Y)

    def x_block(d, s):
        return mod(x - sgn * s, X) if d == 0 else mod(x + sgn * s, X)

    def ring(d, s, k):
        ref = chunk(y_block(d, s), k)
        return copy(ref, ref, y_s.at[d, s, k], y_r.at[d, s, k], y_long if d == 0 else y_short)

    def sib(t):
        ref = g.at[t, :, c]
        return copy(ref, ref, sib_s.at[t], sib_r.at[t], sibling)

    def sib_last(k):
        ref = chunk(y_block(0, 4), k)
        return copy(ref, ref, last_s.at[k], last_r.at[k], sibling)

    def hcopy(d, s):
        ref = hb.at[x_block(d, s)]
        src = ht if s == 0 else ref
        return copy(src, ref, h_s.at[d, s], h_r.at[d, s], x_long if d == 0 else x_short)

    steps = (4, 3)

    def h_step(s):
        for d in (0, 1):
            if s < steps[d]:
                hcopy(d, s).wait_recv()
                if s + 1 < steps[d]:
                    start(hcopy(d, s + 1))

    def sent(d, s, k):
        return s < 3 or (s == 3 and d == k // 2)

    def forward(s, k):
        for d in (0, 1):
            if sent(d, s, k):
                ring(d, s, k).wait_recv()
                if sent(d, s + 1, k):
                    start(ring(d, s + 1, k))

    perm = copy(gt, g.at[x, lax.rem(y, 4), c], perm_s, perm_r, perm_to)
    start(perm)

    loads[0].wait()
    loads[1].wait()
    for b in range(WCOL // BLK):
        cols = slice(b * BLK, (b + 1) * BLK)
        scale = jnp.broadcast_to(sv[b : b + 1, :], (BLK, FFD)).T
        w[h, :, cols] = (cv[:, cols].astype(F32) * scale).astype(BF16)

    def zcopy(k):
        ref = chunk(y, 0)
        return copy(ref, ref, z_s.at[k - 1], z_r.at[k - 1], z_peer[k - 1])

    perm.wait_recv()
    for r in range(1, 4):
        start(zcopy(r))
    for k in range(4):
        if k > 0:
            zcopy(k).wait_recv()
        start(ring(0, 0, k))
        start(ring(1, 0, k))
        if k == 0:
            for d in (0, 1):
                start(hcopy(d, 0))
    start(sib(y))
    w_copy = copy(w.at[h], w.at[h], w_s, w_r, h_peer)
    start(w_copy)
    h_step(0)

    def grad_hidden(t):
        r = lax.dot_general(
            w[0], g[t, 0:2].reshape(WCOL, TOK), (((1,), (0,)), ((), ())), preferred_element_type=F32
        )
        p[t] = r + lax.dot_general(
            w[1], g[t, 2:4].reshape(WCOL, TOK), (((1,), (0,)), ((), ())), preferred_element_type=F32
        )

    def grad_weight(t, first=False):
        for n in range(2):
            r = lax.dot_general(
                hb[t],
                g[t, 2 * n : 2 * n + 2].reshape(WCOL, TOK),
                (((1,), (1,)), ((), ())),
                preferred_element_type=F32,
            )
            if first:
                acc[n] = r
            else:
                acc[n] += r

    def at_distance(s):
        return [y_block(0, s)] if s in (0, 4) else [y_block(0, s), y_block(1, s)]

    half = FFD // 2

    def block_of(idx):
        b = mod(y + (idx + 1) // 2 * (1 if idx % 2 else -1), Y)
        return b, lax.rem(sgn * (b - x) + 2 * X, X)

    def rs(b, r, q, dst, recv, to):
        rows = pl.ds(q * half, half)
        return copy(rs_out.at[b, rows], dst.at[rows], rs_s.at[b, q], recv.at[q], to)

    def to_next(b, r, q):
        nx = mod(x + jnp.where(r <= 4, sgn, -sgn), X)
        return rs(b, r, q, pair_in.at[b], pair_r.at[b], dev(nx, h, zl, y, c))

    def to_owner(b, r, q):
        j = jnp.where(r == 3, 0, jnp.where(r == 6, 1, jnp.where(r == 1, 2, 3)))
        return rs(b, r, q, own_in.at[j], own_r.at[j], dev(b, h, zl, y, c))

    def launch(idx):
        b, r = block_of(idx)
        hand = (r == 4) | (r == 2) | (r == 5)
        for q in range(2):
            rows = pl.ds(q * half, half)

            @pl.when(hand | (r == 7))
            def _():
                rs_out[b, rows] = p[b, rows].astype(BF16)

            @pl.when(hand)
            def _():
                to_next(b, r, q).start()

            @pl.when(r == 7)
            def _():
                to_owner(b, r, q).start()

    def combine(idx):
        b, r = block_of(idx)

        @pl.when((r == 3) | (r == 1) | (r == 6))
        def _():
            for q in range(2):
                rows = pl.ds(q * half, half)
                to_next(b, r, q).wait_recv()
                rs_out[b, rows] = (p[b, rows] + pair_in[b, rows].astype(F32)).astype(BF16)
                to_owner(b, r, q).start()

    for s in range(4):
        for k in range(4):
            forward(s, k)
            if s == 3:
                start(sib_last(k))
        for t in at_distance(s + 1) if s < 3 else []:
            start(sib(t))
        if s < 3:
            h_step(s + 1)
        if s == 1:
            w_copy.wait_recv()
            for t in at_distance(0) + at_distance(1):
                sib(t).wait_recv()
                grad_hidden(t)
            for idx in (0, 1, 2):
                launch(idx)
        if s >= 2:
            for t in at_distance(s):
                sib(t).wait_recv()
                grad_hidden(t)
            for idx in (2 * s - 1, 2 * s):
                launch(idx)
        if s == 2:
            loads[2].wait()
            grad_weight(y, True)
            for t in at_distance(1) + at_distance(2):
                grad_weight(t)
        if s == 3:
            for idx in (0, 1, 2):
                combine(idx)
            for t in at_distance(3):
                grad_weight(t)
    last = y_block(0, 4)
    for k in range(4):
        sib_last(k).wait_recv()
    grad_hidden(last)
    launch(7)
    grad_weight(last)
    gw_out[...] = acc[1 - h].astype(BF16)
    gw_copy = copy(gw_out, gw_in, gw_s, gw_r, h_peer)
    start(gw_copy)
    for idx in (3, 4, 5, 6, 7):
        combine(idx)
    for q in range(2):
        rows = pl.ds(q * half, half)
        v = p[x, rows]
        for j in (3, 2, 1, 0):
            rs(x, 0, q, own_in.at[j], own_r.at[j], x_long).wait_recv()
            v = v + own_in[j, rows].astype(F32)
        ght[rows] = v.astype(BF16)
    gw_copy.wait_recv()
    gw[...] = acc[h] + gw_in[...].astype(F32)

    for idx in range(8):
        b, r = block_of(idx)

        @pl.when(r > 0)
        def _():
            for q in range(2):
                to_next(b, r, q).wait_send()

    for cp in sends:
        cp.wait_send()


def shards(hidden, grad_out, codes, scales):
    vmem = pl.BlockSpec(memory_space=pltpu.VMEM)
    hbm = pl.BlockSpec(memory_space=pltpu.HBM)
    dma = pltpu.SemaphoreType.DMA
    ght, gw = pl.pallas_call(
        kernel,
        out_shape=(
            jax.ShapeDtypeStruct((FFD, TOK), BF16),
            jax.ShapeDtypeStruct((FFD, WCOL), F32),
        ),
        in_specs=[hbm] * 4,
        out_specs=(vmem, vmem),
        scratch_shapes=[
            pltpu.VMEM((Y, 4, 2, GCOL, TOK), BF16),
            pltpu.VMEM((X, FFD, TOK), BF16),
            pltpu.VMEM((FFD, WCOL), BF16),
            pltpu.VMEM((WCOL // BLK, FFD), F32),
            pltpu.VMEM((2, FFD, WCOL), BF16),
            pltpu.VMEM((2, FFD, WCOL), F32),
            pltpu.VMEM((X, FFD, TOK), F32),
            pltpu.VMEM((X, FFD, TOK), BF16),
            pltpu.VMEM((X, FFD, TOK), BF16),
            pltpu.VMEM((4, FFD, TOK), BF16),
            pltpu.VMEM((FFD, WCOL), BF16),
            pltpu.VMEM((FFD, WCOL), BF16),
            dma((3,)),
            dma, dma,
            dma((3,)), dma((3,)),
            dma((2, 4, 4)), dma((2, 4, 4)),
            dma((8,)), dma((8,)),
            dma((4,)), dma((4,)),
            dma((2, 4)), dma((2, 4)),
            dma, dma,
            dma((X, 2)), dma((X, 2)), dma((4, 2)),
            dma, dma,
        ],
        compiler_params=pltpu.CompilerParams(
            collective_id=0, has_side_effects=True, vmem_limit_bytes=32 * 2**20
        ),
        name="fused",
    )(*[pltpu.with_memory_space_constraint(v, pltpu.HBM) for v in (hidden.T, grad_out.T, codes, scales.T)])
    return ght.T, gw


def solution(mesh):
    return jax.shard_map(
        shards,
        mesh=mesh,
        in_specs=(
            P("inner", "outer"),
            P("inner", "outer"),
            P("outer", "inner"),
            P("outer", "inner"),
        ),
        out_specs=(P("inner", "outer"), P("outer", "inner")),
        check_vma=False,
    )
```

```python
import jax
import jax.numpy as jnp
from jax import lax
from jax.experimental import pallas as pl
from jax.experimental.pallas import tpu as pltpu
from jax.sharding import PartitionSpec as P

BLK = 128
X, HZ, ZL, Y = 8, 2, 4, 8
TOK, FFD, GCOL, WCOL = 256, 224, 96, 384
MESH = pl.DeviceIdType.MESH
F32, BF16 = jnp.float32, jnp.bfloat16


def kernel(
    ht, gt, codes, scales, ght, gw,
    g, hb, cv, sv, w, acc, p, rs_out, pair_in, own_in, gw_out, gw_in,
    in_s, perm_s, perm_r, z_s, z_r, y_s, y_r, sib_s, sib_r, last_s, last_r, h_s, h_r, w_s, w_r, rs_s, pair_r, own_r, gw_s, gw_r,
):
    o = lax.axis_index("outer")
    i = lax.axis_index("inner")
    c = lax.rem(o, 2)
    y = lax.rem(o // 2, Y)
    zl = o // (2 * Y)
    x = i // HZ
    h = lax.rem(i, HZ)
    sgn = 1 - 2 * c

    def dev(x_, h_, zl_, y_, c_):
        return {"outer": zl_ * (2 * Y) + y_ * 2 + c_, "inner": x_ * HZ + h_}

    def mod(a, n):
        return lax.rem(a + n, n)

    perm_to = dev(2 * zl + y // 4, h, mod(lax.rem(y, 4) + 2, 4), x, c)
    perm_from = dev(y, h, x // 2, lax.rem(x, 2) * 4 + mod(zl + 2, 4), c)
    z_peer = [dev(x, h, mod(zl + r, ZL), y, c) for r in range(1, ZL)]
    sibling = dev(x, h, zl, y, 1 - c)
    y_long, y_short = dev(x, h, zl, mod(y + sgn, Y), c), dev(x, h, zl, mod(y - sgn, Y), c)
    x_long, x_short = dev(mod(x + sgn, X), h, zl, y, c), dev(mod(x - sgn, X), h, zl, y, c)
    h_peer = dev(x, 1 - h, zl, y, c)
    x_far = [dev(mod(x + n * sgn, X), h, zl, y, c) for n in (3, -3, 2, -2)]
    peers = [perm_to, perm_from, *z_peer, sibling, y_long, y_short, x_long, x_short, *x_far, h_peer]

    barrier = pltpu.get_barrier_semaphore()
    for peer in peers:
        pl.semaphore_signal(barrier, inc=1, device_id=peer, device_id_type=MESH)

    loads = [
        pltpu.make_async_copy(codes, cv, in_s.at[0]),
        pltpu.make_async_copy(scales, sv, in_s.at[1]),
        pltpu.make_async_copy(ht, hb.at[x], in_s.at[2]),
    ]
    for load in loads:
        load.start()

    pl.semaphore_wait(barrier, len(peers))

    sends = []

    def copy(src, dst, s, r, to):
        return pltpu.make_async_remote_copy(
            src_ref=src, dst_ref=dst, send_sem=s, recv_sem=r, device_id=to, device_id_type=MESH
        )

    def start(cp):
        cp.start()
        sends.append(cp)

    def chunk(t, k):
        return g.at[t, mod(zl + 2 - k, 4), c]

    def y_block(d, s):
        return mod(y - sgn * s, Y) if d == 0 else mod(y + sgn * s, Y)

    def x_block(d, s):
        return mod(x - sgn * s, X) if d == 0 else mod(x + sgn * s, X)

    def ring(d, s, k):
        ref = chunk(y_block(d, s), k)
        return copy(ref, ref, y_s.at[d, s, k], y_r.at[d, s, k], y_long if d == 0 else y_short)

    def sib(t):
        ref = g.at[t, :, c]
        return copy(ref, ref, sib_s.at[t], sib_r.at[t], sibling)

    def sib_last(k):
        ref = chunk(y_block(0, 4), k)
        return copy(ref, ref, last_s.at[k], last_r.at[k], sibling)

    def hcopy(d, s):
        ref = hb.at[x_block(d, s)]
        src = ht if s == 0 else ref
        return copy(src, ref, h_s.at[d, s], h_r.at[d, s], x_long if d == 0 else x_short)

    steps = (4, 3)

    def h_step(s):
        for d in (0, 1):
            if s < steps[d]:
                hcopy(d, s).wait_recv()
                if s + 1 < steps[d]:
                    start(hcopy(d, s + 1))

    def sent(d, s, k):
        return s < 3 or (s == 3 and d == k // 2)

    def forward(s, k):
        for d in (0, 1):
            if sent(d, s, k):
                ring(d, s, k).wait_recv()
                if sent(d, s + 1, k):
                    start(ring(d, s + 1, k))

    perm = copy(gt, g.at[x, lax.rem(y, 4), c], perm_s, perm_r, perm_to)
    start(perm)

    loads[0].wait()
    loads[1].wait()
    for b in range(WCOL // BLK):
        cols = slice(b * BLK, (b + 1) * BLK)
        scale = jnp.broadcast_to(sv[b : b + 1, :], (BLK, FFD)).T
        w[h, :, cols] = (cv[:, cols].astype(F32) * scale).astype(BF16)

    def zcopy(k):
        ref = chunk(y, 0)
        return copy(ref, ref, z_s.at[k - 1], z_r.at[k - 1], z_peer[k - 1])

    perm.wait_recv()
    for r in range(1, 4):
        start(zcopy(r))
    for k in range(4):
        if k > 0:
            zcopy(k).wait_recv()
        start(ring(0, 0, k))
        start(ring(1, 0, k))
        if k == 0:
            for d in (0, 1):
                start(hcopy(d, 0))
    start(sib(y))
    w_copy = copy(w.at[h], w.at[h], w_s, w_r, h_peer)
    start(w_copy)
    h_step(0)

    def grad_hidden(t):
        r = lax.dot_general(
            w[0], g[t, 0:2].reshape(WCOL, TOK), (((1,), (0,)), ((), ())), preferred_element_type=F32
        )
        p[t] = r + lax.dot_general(
            w[1], g[t, 2:4].reshape(WCOL, TOK), (((1,), (0,)), ((), ())), preferred_element_type=F32
        )

    def grad_weight(t, first=False):
        for n in range(2):
            r = lax.dot_general(
                hb[t],
                g[t, 2 * n : 2 * n + 2].reshape(WCOL, TOK),
                (((1,), (1,)), ((), ())),
                preferred_element_type=F32,
            )
            if first:
                acc[n] = r
            else:
                acc[n] += r

    def at_distance(s):
        return [y_block(0, s)] if s in (0, 4) else [y_block(0, s), y_block(1, s)]

    half = FFD // 2

    def block_of(idx):
        b = mod(y + (idx + 1) // 2 * (1 if idx % 2 else -1), Y)
        return b, lax.rem(sgn * (b - x) + 2 * X, X)

    def rs(b, r, q, dst, recv, to):
        rows = pl.ds(q * half, half)
        return copy(rs_out.at[b, rows], dst.at[rows], rs_s.at[b, q], recv.at[q], to)

    def to_next(b, r, q):
        nx = mod(x + jnp.where(r <= 4, sgn, -sgn), X)
        return rs(b, r, q, pair_in.at[b], pair_r.at[b], dev(nx, h, zl, y, c))

    def to_owner(b, r, q):
        j = jnp.where(r == 3, 0, jnp.where(r == 6, 1, jnp.where(r == 1, 2, 3)))
        return rs(b, r, q, own_in.at[j], own_r.at[j], dev(b, h, zl, y, c))

    def launch(idx):
        b, r = block_of(idx)
        hand = (r == 4) | (r == 2) | (r == 5)
        for q in range(2):
            rows = pl.ds(q * half, half)

            @pl.when(hand | (r == 7))
            def _():
                rs_out[b, rows] = p[b, rows].astype(BF16)

            @pl.when(hand)
            def _():
                to_next(b, r, q).start()

            @pl.when(r == 7)
            def _():
                to_owner(b, r, q).start()

    def combine(idx):
        b, r = block_of(idx)

        @pl.when((r == 3) | (r == 1) | (r == 6))
        def _():
            for q in range(2):
                rows = pl.ds(q * half, half)
                to_next(b, r, q).wait_recv()
                rs_out[b, rows] = (p[b, rows] + pair_in[b, rows].astype(F32)).astype(BF16)
                to_owner(b, r, q).start()

    for s in range(4):
        for k in range(4):
            forward(s, k)
            if s == 3:
                start(sib_last(k))
        for t in at_distance(s + 1) if s < 3 else []:
            start(sib(t))
        if s < 3:
            h_step(s + 1)
        if s == 1:
            w_copy.wait_recv()
            for t in at_distance(0) + at_distance(1):
                sib(t).wait_recv()
                grad_hidden(t)
            for idx in (0, 1, 2):
                launch(idx)
        if s >= 2:
            for t in at_distance(s):
                sib(t).wait_recv()
                grad_hidden(t)
            for idx in (2 * s - 1, 2 * s):
                launch(idx)
        if s == 2:
            loads[2].wait()
            grad_weight(y, True)
            for t in at_distance(1) + at_distance(2):
                grad_weight(t)
        if s == 3:
            for t in at_distance(3):
                grad_weight(t)
            for idx in (0, 1, 2):
                combine(idx)
    last = y_block(0, 4)
    for k in range(4):
        sib_last(k).wait_recv()
    grad_weight(last)
    gw_out[...] = acc[1 - h].astype(BF16)
    gw_copy = copy(gw_out, gw_in, gw_s, gw_r, h_peer)
    start(gw_copy)
    grad_hidden(last)
    launch(7)
    for idx in (3, 4, 5, 6, 7):
        combine(idx)
    for q in range(2):
        rows = pl.ds(q * half, half)
        v = p[x, rows]
        for j in (3, 2, 1, 0):
            rs(x, 0, q, own_in.at[j], own_r.at[j], x_long).wait_recv()
            v = v + own_in[j, rows].astype(F32)
        ght[rows] = v.astype(BF16)
    gw_copy.wait_recv()
    gw[...] = acc[h] + gw_in[...].astype(F32)

    for idx in range(8):
        b, r = block_of(idx)

        @pl.when(r > 0)
        def _():
            for q in range(2):
                to_next(b, r, q).wait_send()

    for cp in sends:
        cp.wait_send()


def shards(hidden, grad_out, codes, scales):
    vmem = pl.BlockSpec(memory_space=pltpu.VMEM)
    hbm = pl.BlockSpec(memory_space=pltpu.HBM)
    dma = pltpu.SemaphoreType.DMA
    ght, gw = pl.pallas_call(
        kernel,
        out_shape=(
            jax.ShapeDtypeStruct((FFD, TOK), BF16),
            jax.ShapeDtypeStruct((FFD, WCOL), F32),
        ),
        in_specs=[hbm] * 4,
        out_specs=(vmem, vmem),
        scratch_shapes=[
            pltpu.VMEM((Y, 4, 2, GCOL, TOK), BF16),
            pltpu.VMEM((X, FFD, TOK), BF16),
            pltpu.VMEM((FFD, WCOL), BF16),
            pltpu.VMEM((WCOL // BLK, FFD), F32),
            pltpu.VMEM((2, FFD, WCOL), BF16),
            pltpu.VMEM((2, FFD, WCOL), F32),
            pltpu.VMEM((X, FFD, TOK), F32),
            pltpu.VMEM((X, FFD, TOK), BF16),
            pltpu.VMEM((X, FFD, TOK), BF16),
            pltpu.VMEM((4, FFD, TOK), BF16),
            pltpu.VMEM((FFD, WCOL), BF16),
            pltpu.VMEM((FFD, WCOL), BF16),
            dma((3,)),
            dma, dma,
            dma((3,)), dma((3,)),
            dma((2, 4, 4)), dma((2, 4, 4)),
            dma((8,)), dma((8,)),
            dma((4,)), dma((4,)),
            dma((2, 4)), dma((2, 4)),
            dma, dma,
            dma((X, 2)), dma((X, 2)), dma((4, 2)),
            dma, dma,
        ],
        compiler_params=pltpu.CompilerParams(
            collective_id=0, has_side_effects=True, vmem_limit_bytes=32 * 2**20
        ),
        name="fused",
    )(*[pltpu.with_memory_space_constraint(v, pltpu.HBM) for v in (hidden.T, grad_out.T, codes, scales.T)])
    return ght.T, gw


def solution(mesh):
    return jax.shard_map(
        shards,
        mesh=mesh,
        in_specs=(
            P("inner", "outer"),
            P("inner", "outer"),
            P("outer", "inner"),
            P("outer", "inner"),
        ),
        out_specs=(P("inner", "outer"), P("outer", "inner")),
        check_vma=False,
    )
```
